256 devices in a mesh: loop: 64 (over y_hi, x, z), rep: 4 (over y_lo, core).
Axes of the slice: x: 4, y: 4 (y_hi: 2, y_lo: 2; y = y_hi * 2 + y_lo), z: 8, core: 2. Of those that a mesh axis runs over, the one named last changes fastest.
Arguments:
- teacher_acts: bfloat16 [32768, 16384], P('loop', 'rep'), may hold values from -6 to 6
- gate_weight: bfloat16 [16384, 8192], P('rep', 'loop'), may hold values from -0.046875 to 0.046875
- up_weight: bfloat16 [16384, 8192], P('rep', 'loop'), may hold values from -0.046875 to 0.046875
- down_weight: bfloat16 [8192, 16384], P('loop', 'rep'), may hold values from -0.25 to 0.25
Outputs:
- teacher_out: bfloat16 [32768, 16384], P('loop', 'rep')
The draws below stay inside these ranges and needn't reach their ends.
All inputs are finite; a program needn't handle non-finite values.
Results may differ from the reference program's by a relative error of at most 0.0049.
Values may be sent and summed in bfloat16 or wider, within the bound.
A program may use at most 128 MiB of HBM per device.

```python
import jax
import jax.numpy as jnp
from jax import lax

DT = 16384
CH = 128
STEPS = 4
FF = 8192
TT = 512
TOKENS_T = 32768
N_LOOP = 64


def block_scale(rng, shape, cuts, low, largest):
    loudness, own = 1.0, jax.random.fold_in(rng, 6)
    for position, shards_of in cuts:
        steps = jnp.exp(jax.random.uniform(jax.random.fold_in(own, position), (shards_of,), jnp.float32, low / len(cuts), largest / len(cuts)))
        loudness = loudness * jnp.repeat(steps, shape[position] // shards_of).reshape([-1 if axis == position else 1 for axis in range(len(shape))])
    return loudness


def bell_draw(key, extent, deviation, most, pieces=(), kind=jnp.bfloat16):
    values = deviation * jax.random.normal(key, extent, jnp.float32)
    if pieces:
        values = values * block_scale(key, extent, pieces, -0.22, 0.18)
    return jnp.clip(values, -most, most).astype(kind)


def setup_inputs(seed: int = 0) -> dict:
    splits = jax.random.split(jax.random.key(seed), 5)
    teacher_acts = bell_draw(splits[0], (TOKENS_T, DT), 1.0, 6.0, ((0, 64), (1, 4)))
    gate_weight = bell_draw(splits[1], (DT, FF), DT ** -0.5, 0.046875, ((0, 4), (1, 64)))
    up_weight = bell_draw(splits[2], (DT, FF), DT ** -0.5, 0.046875, ((0, 4), (1, 64)))
    down_weight = bell_draw(splits[3], (FF, DT), (STEPS * CH) ** -0.5, 0.25, ((0, 64), (1, 4)))
    return {"teacher_acts": teacher_acts, "gate_weight": gate_weight, "up_weight": up_weight, "down_weight": down_weight}


def reference(teacher_acts, gate_weight, up_weight, down_weight):
    blocks = teacher_acts.reshape(N_LOOP, TT, DT)

    def one_block(inputs):
        block, index = inputs
        total = jnp.zeros((TT, DT), jnp.float32)
        for step in range(STEPS):
            group = ((index - step) % N_LOOP).astype(jnp.int32)
            start = (group * CH).astype(jnp.int32)
            gate_part = lax.dynamic_slice_in_dim(gate_weight, start, CH, 1)
            up_part = lax.dynamic_slice_in_dim(up_weight, start, CH, 1)
            down_part = lax.dynamic_slice_in_dim(down_weight, start, CH, 0)
            gate = jnp.dot(block, gate_part, preferred_element_type=jnp.float32)
            upval = jnp.dot(block, up_part, preferred_element_type=jnp.float32)
            hidden = (jax.nn.silu(gate) * upval).astype(jnp.bfloat16)
            total = total + jnp.dot(hidden, down_part, preferred_element_type=jnp.float32)
        return total.astype(jnp.bfloat16)

    outputs = lax.map(one_block, (blocks, jnp.arange(N_LOOP, dtype=jnp.int32)))
    return outputs.reshape(TOKENS_T, DT)
```

```python
import functools

import jax
import jax.numpy as jnp
from jax import lax
from jax.experimental import pallas as pl
from jax.experimental.pallas import tpu as pltpu
from jax.sharding import PartitionSpec as P

MESH = pl.DeviceIdType.MESH
NQ = 4
NB = 4
ND = 4
NE = 8
F32 = jnp.float32
BF16 = jnp.bfloat16


def dot(a, b):
    return jnp.dot(a, b, preferred_element_type=F32)


def silu_times(gate, up):
    return gate / (1.0 + jnp.exp(-gate)) * up


def kernel(
    n,
    near,
    acts,
    gate,
    up,
    down,
    out,
    a_own,
    a_1,
    a_2,
    w_own,
    w_1,
    w_2,
    dn,
    hid,
    part,
    part_in,
    far_part,
    far_in,
    acc,
    stage,
    stage_in,
    carry,
    carry_in,
    fwd,
    o_buf,
    send_sem,
    recv_sem,
    local_sem,
):
    l, r = lax.axis_index("loop"), lax.axis_index("rep")
    ahead = (lax.rem(l + 1, n), r)
    behind = (lax.rem(l + n - 1, n), r)
    mates = [(l, lax.rem(r + o, NQ)) for o in range(1, NQ)]
    rows, feats = acts.shape
    width = gate.shape[1]
    far = feats - near
    rb = rows // NB
    rq = rb // NQ
    qr = rows // NQ
    started = []

    def remote(src, dst, to):
        i = len(started)
        c = pltpu.make_async_remote_copy(
            src_ref=src,
            dst_ref=dst,
            send_sem=send_sem.at[i],
            recv_sem=recv_sem.at[i],
            device_id=to,
            device_id_type=MESH,
        )
        c.start()
        started.append(c)
        return c

    loads = [
        pltpu.make_async_copy(acts, a_own, local_sem.at[0]),
        pltpu.make_async_copy(gate, w_own.at[0], local_sem.at[1]),
        pltpu.make_async_copy(up, w_own.at[1], local_sem.at[2]),
        pltpu.make_async_copy(down, dn.at[pl.ds(0, width)], local_sem.at[3]),
    ]
    for c in loads:
        c.start()

    barrier = pltpu.get_barrier_semaphore()
    peers = [ahead, behind] + mates
    for p in peers:
        pl.semaphore_signal(barrier, inc=1, device_id=p, device_id_type=MESH)
    pl.semaphore_wait(barrier, len(peers))

    nears, fars = pl.ds(0, near), pl.ds(near, far)

    w1_far = [
        remote(src.at[fars], w_1.at[h, fars], ahead) for h, src in enumerate((gate, up))
    ]
    a1_near = [
        remote(acts.at[pl.ds(i * rb, rb), nears], a_1.at[pl.ds(i * rb, rb), nears], behind)
        for i in range(NB)
    ]
    w1_near = [
        remote(src.at[nears], w_1.at[h, nears], ahead) for h, src in enumerate((gate, up))
    ]

    def weights(ref, at, kc):
        at = pl.multiple_of(at, 128)
        return [ref[0, pl.ds(at, kc), :], ref[1, pl.ds(at, kc), :]]

    def whole(a_ref, w_ref, count, acc_ref):
        kc = 256
        acc_ref[...] = jnp.zeros_like(acc_ref)

        def step(k, _):
            at = pl.multiple_of(k * kc, kc)
            w = jnp.concatenate(weights(w_ref, at, kc), axis=1)
            acc_ref[...] += dot(a_ref[:, pl.ds(at, kc)], w)
            return 0

        lax.fori_loop(0, count // kc, step, 0)

    def scatter(buf, into):
        return [remote(buf.at[to[1]], into.at[o], to) for o, to in enumerate(mates)]

    def own_pair(s, w_ref):
        whole(a_own, w_ref, feats, acc)
        for q in range(NQ):
            part[s, q] = acc[q * qr : (q + 1) * qr, :]
        return scatter(part.at[s], part_in.at[s])

    def own_hidden(s, copies):
        for c in copies:
            c.wait_recv()
        total = part[s, r] + part_in[s, 0] + part_in[s, 1] + part_in[s, 2]
        value = silu_times(total[:, :width], total[:, width:])
        at = (pl.ds(pl.multiple_of(r * qr, qr), qr), pl.ds(s * width, width))
        hid[at] = value.astype(BF16)
        return [remote(hid.at[at], hid.at[at], to) for to in mates]

    gathers = []
    for c in loads:
        c.wait()
    copies = own_pair(0, w_own)
    gathers += own_hidden(0, copies)

    a2 = []

    def relay_a(i):
        a1_near[i].wait_recv()
        at = (pl.ds(i * rb, rb), nears)
        a2.append(remote(a_1.at[at], a_2.at[pl.ds(i * rb, rb)], behind))

    relay_a(0)
    relay_a(1)
    relay_a(2)
    w2_far = []
    for h in range(2):
        w1_far[h].wait_recv()
        w2_far.append(remote(w_1.at[h, fars], w_2.at[h], ahead))
    relay_a(3)
    a1_far = [
        remote(acts.at[pl.ds(i * rb, rb), fars], a_1.at[pl.ds(i * rb, rb), fars], behind)
        for i in range(NB)
    ]
    for c in w1_near:
        c.wait_recv()
    copies = own_pair(1, w_1)
    gathers += own_hidden(1, copies)
    whole(a_1, w_1, near, acc)

    d1 = []
    for i in range(NB):
        if i == NB - 1:
            for j in range(ND):
                at = pl.ds(j * (feats // ND), feats // ND)
                d1.append(remote(down.at[:, at], dn.at[pl.ds(width, width), at], ahead))
        a2[i].wait_recv()
        kc = 256

        def near_step(k, total, i=i):
            at = pl.multiple_of(k * kc, kc)
            w = jnp.concatenate(weights(w_1, at, kc), axis=1)
            return total + dot(a_2[pl.ds(i * rb, rb), pl.ds(at, kc)], w)

        total = lax.fori_loop(0, near // kc, near_step, jnp.zeros((rb, 2 * width), F32))
        for q in range(NQ):
            far_part[q, i] = total[q * rq : (q + 1) * rq, :]
    copies = scatter(far_part, far_in)
    for c in copies:
        c.wait_recv()
    carry[...] = far_part[r] + far_in[0] + far_in[1] + far_in[2]
    carried = remote(carry, carry_in, ahead)

    for c in w2_far:
        c.wait_recv()

    d2, d3 = [], []

    def relay_d2(j):
        d1[j].wait_recv()
        at = pl.ds(j * (feats // ND), feats // ND)
        d2.append(
            remote(dn.at[pl.ds(width, width), at], dn.at[pl.ds(2 * width, width), at], ahead)
        )

    def relay_d3(j):
        d2[j].wait_recv()
        for e in range(j * NE // ND, (j + 1) * NE // ND):
            at = pl.ds(e * (feats // NE), feats // NE)
            d3.append(
                remote(
                    dn.at[pl.ds(2 * width, width), at],
                    dn.at[pl.ds(3 * width, width), at],
                    ahead,
                )
            )

    later = pl.ds(2 * width, 2 * width)

    def stage_rows(i):
        a1_far[i].wait_recv()
        kc = 256

        def far_step(k, total):
            at = pl.multiple_of(k * kc, kc)
            there = pl.multiple_of(near + at, kc)
            w = jnp.concatenate(weights(w_1, there, kc) + weights(w_2, at, kc), axis=1)
            return total + dot(a_1[pl.ds(i * rb, rb), pl.ds(there, kc)], w)

        total = lax.fori_loop(0, far // kc, far_step, jnp.zeros((rb, 4 * width), F32))
        for q in range(NQ):
            at = pl.ds(q * rq, rq)
            mine = total[q * rq : (q + 1) * rq, :]
            stage[i, q, :, : 2 * width] = mine[:, : 2 * width] + acc[pl.ds(i * rb + q * rq, rq), :]
            stage[i, q, :, 2 * width :] = mine[:, 2 * width :]
        copies = scatter(stage.at[i], stage_in.at[i])
        if i == 0:
            carried.wait_recv()
        for c in copies:
            c.wait_recv()
        total = stage[i, r] + stage_in[i, 0] + stage_in[i, 1] + stage_in[i, 2]
        one, two = total[:, : 2 * width], total[:, 2 * width :] + carry_in[i]
        fwd[i, :, :width] = silu_times(one[:, :width], one[:, width:]).astype(BF16)
        fwd[i, :, width:] = silu_times(two[:, :width], two[:, width:]).astype(BF16)
        at = (pl.ds(pl.multiple_of(i * rb + r * rq, rq), rq), later)
        sent = remote(fwd.at[i], hid.at[at], ahead)
        sent.wait_recv()
        return [remote(hid.at[at], hid.at[at], to) for to in mates]

    gathers += stage_rows(0)
    relay_d2(0)
    relay_d2(1)
    relay_d2(2)
    gathers += stage_rows(1)
    relay_d2(3)
    relay_d3(0)
    relay_d3(1)
    gathers += stage_rows(2)
    relay_d3(2)
    relay_d3(3)
    gathers += stage_rows(3)
    for c in gathers:
        c.wait_recv()

    stores = []
    for e in range(NE):
        d3[e].wait_recv()
        cols = feats // NE
        at = pl.ds(e * cols, cols)
        o_buf[:, at] = dot(hid[...], dn[:, at]).astype(BF16)
        c = pltpu.make_async_copy(o_buf.at[:, at], out.at[:, at], local_sem.at[4 + e])
        c.start()
        stores.append(c)
    for c in started:
        c.wait_send()
    for c in stores:
        c.wait()


COPIES = 96


def body(n, near, acts, gate, up, down):
    rows, feats = acts.shape
    width = gate.shape[1]
    far = feats - near
    rb, qr = rows // NB, rows // NQ
    rq = rb // NQ
    any_space = pl.BlockSpec(memory_space=pl.ANY)
    vmem = pltpu.VMEM
    return pl.pallas_call(
        functools.partial(kernel, n, near),
        out_shape=jax.ShapeDtypeStruct((rows, feats), BF16),
        in_specs=[any_space] * 4,
        out_specs=any_space,
        scratch_shapes=[
            vmem((rows, feats), BF16),
            vmem((rows, feats), BF16),
            vmem((rows, near), BF16),
            vmem((2, feats, width), BF16),
            vmem((2, feats, width), BF16),
            vmem((2, far, width), BF16),
            vmem((4 * width, feats), BF16),
            vmem((rows, 4 * width), BF16),
            vmem((2, NQ, qr, 2 * width), F32),
            vmem((2, NQ - 1, qr, 2 * width), F32),
            vmem((NQ, NB, rq, 2 * width), F32),
            vmem((NQ - 1, NB, rq, 2 * width), F32),
            vmem((rows, 2 * width), F32),
            vmem((NB, NQ, rq, 4 * width), F32),
            vmem((NB, NQ - 1, rq, 4 * width), F32),
            vmem((NB, rq, 2 * width), F32),
            vmem((NB, rq, 2 * width), F32),
            vmem((NB, rq, 2 * width), BF16),
            vmem((rows, feats), BF16),
            pltpu.SemaphoreType.DMA((COPIES,)),
            pltpu.SemaphoreType.DMA((COPIES,)),
            pltpu.SemaphoreType.DMA((4 + NE,)),
        ],
        compiler_params=pltpu.CompilerParams(
            collective_id=0, has_side_effects=True, vmem_limit_bytes=56 * 2**20
        ),
    )(acts, gate, up, down)


NEAR = 6


def solution(mesh):
    n = mesh.shape["loop"]
    placed = (P("loop", "rep"), P("rep", "loop"), P("rep", "loop"), P("loop", "rep"))

    def step(acts, gate, up, down):
        return body(n, acts.shape[1] // 16 * NEAR, acts, gate, up, down)

    return jax.shard_map(
        step, mesh=mesh, in_specs=placed, out_specs=P("loop", "rep"), check_vma=False
    )
```

```python
import functools

import jax
import jax.numpy as jnp
from jax import lax
from jax.experimental import pallas as pl
from jax.experimental.pallas import tpu as pltpu
from jax.sharding import PartitionSpec as P

MESH = pl.DeviceIdType.MESH
NEAR = 5
NB = 4
NA = 16
ND = 8
WINDOW = 3
CROSS = 3
LAG = 5
COPIES = 192
F32 = jnp.float32
BF16 = jnp.bfloat16


def dot(a, b):
    return jnp.dot(a, b, preferred_element_type=F32)


def silu_times(gate, up):
    return gate / (1.0 + jnp.exp(-gate)) * up


def kernel(
    n,
    near,
    acts,
    gate,
    up,
    down,
    out,
    a_own,
    a_1,
    a_2,
    w_own,
    w_1,
    w_2,
    dn,
    hid,
    part,
    part_in,
    half_in,
    far_part,
    far_in,
    far_half,
    acc,
    stage,
    stage_in,
    stage_half,
    carry,
    carry_in,
    fwd,
    o_buf,
    v_w1,
    v_w2,
    v_d,
    v_a1,
    v_a2,
    v_carry,
    v_fwd,
    send_sem,
    recv_sem,
    pass_sem,
    on_sem,
    local_sem,
):
    l, r = lax.axis_index("loop"), lax.axis_index("rep")
    core, y = lax.rem(r, 2), lax.div(r, 2)
    ahead = (lax.rem(l + 1, n), r)
    behind = (lax.rem(l + n - 1, n), r)
    half = n // 2
    first, final = lax.rem(l, half) == 0, lax.rem(l, half) == half - 1
    other = lax.rem(r + 2, 4)
    partner = (lax.rem(l + half, n), other)
    ahead_via = (lax.rem(l + 1 + half, n), other)
    behind_via = (lax.rem(l + n - 1 + half, n), other)
    twin = (l, r + 1 - 2 * core)
    across = (l, lax.rem(r + 2, 4))
    rows, feats = acts.shape
    width = gate.shape[1]
    far = feats - near
    rb = rows // NB
    ra = rows // NA
    rq = rb // 4
    qr = rows // 4
    mine = 2 * core + y
    started = []

    def remote(src, dst, to):
        i = len(started)
        c = pltpu.make_async_remote_copy(
            src_ref=src,
            dst_ref=dst,
            send_sem=send_sem.at[i],
            recv_sem=recv_sem.at[i],
            device_id=to,
            device_id_type=MESH,
        )
        c.start()
        started.append(c)
        return c

    class Hop:
        def __init__(self, src, dst, by, to, on=None):
            self.i = i = len(started)
            self.by, self.on = by, dst if on is None else on
            self.end, self.via = (final, first) if to is ahead else (first, final)
            self.id = id(self)
            whole = pltpu.make_async_remote_copy(
                src_ref=src,
                dst_ref=dst,
                send_sem=send_sem.at[i],
                recv_sem=recv_sem.at[i],
                device_id=to,
                device_id_type=MESH,
            )
            leg = pltpu.make_async_remote_copy(
                src_ref=src,
                dst_ref=by,
                send_sem=send_sem.at[i],
                recv_sem=pass_sem.at[i],
                device_id=ahead_via if to is ahead else behind_via,
                device_id_type=MESH,
            )
            self.whole, self.leg = whole, leg
            pl.when(self.end)(leg.start)
            pl.when(jnp.logical_not(self.end))(whole.start)
            started.append(self)
            hops.append(self)

        def pass_on(self):
            if self in passed:
                return
            passed.append(self)
            second = pltpu.make_async_remote_copy(
                src_ref=self.by,
                dst_ref=self.on,
                send_sem=on_sem.at[self.i],
                recv_sem=recv_sem.at[self.i],
                device_id=partner,
                device_id_type=MESH,
            )
            self.second = second

            @pl.when(self.via)
            def _():
                self.leg.wait_recv()
                second.start()

        def wait_send(self):
            self.whole.wait_send()

        def wait_recv(self):
            self.whole.wait_recv()

    hops, passed = [], []
    here = set()

    def arrive(c):
        if id(c) not in here:
            here.add(id(c))
            c.wait_recv()

    loads = [
        pltpu.make_async_copy(acts, a_own, local_sem.at[0]),
        pltpu.make_async_copy(gate, w_own.at[0], local_sem.at[1]),
        pltpu.make_async_copy(up, w_own.at[1], local_sem.at[2]),
        pltpu.make_async_copy(down, dn.at[pl.ds(0, width)], local_sem.at[3]),
    ]
    for c in loads:
        c.start()

    barrier = pltpu.get_barrier_semaphore()
    def greet(p):
        pl.semaphore_signal(barrier, inc=1, device_id=p, device_id_type=MESH)

    def choose(cond, one, two):
        return tuple(jnp.where(cond, a, b) for a, b in zip(one, two))

    for p in (choose(final, ahead_via, ahead), choose(first, behind_via, behind), twin, across):
        greet(p)

    @pl.when(jnp.logical_or(first, final))
    def _():
        greet(partner)
        pl.semaphore_wait(barrier, 5)

    @pl.when(jnp.logical_not(jnp.logical_or(first, final)))
    def _():
        pl.semaphore_wait(barrier, 4)

    landed = WINDOW + 1
    crossed = landed + CROSS
    unit = feats * width // ND
    kw = unit // (2 * width)
    w1, w2, d1, d2, d3 = {}, {}, {}, {}, {}
    a1n, a2, a1f = {}, {}, {}

    def send_w(at):
        def go():
            ds = pl.ds(at, kw)
            w1[at] = [
                Hop(s.at[ds], w_1.at[h, ds], v_w1.at[h, ds], ahead) for h, s in enumerate((gate, up))
            ]
            return w1[at]

        return kw * 2 * width / unit, go

    def relay_w(at):
        def go():
            for c in w1[at]:
                arrive(c)
            src, dst = pl.ds(at, kw), pl.ds(at - near, kw)
            w2[at] = [
                Hop(w_1.at[h, src], w_2.at[h, dst], v_w2.at[h, dst], ahead) for h in range(2)
            ]
            return w2[at]

        return kw * 2 * width / unit, go

    def send_d(j):
        def go():
            at = pl.ds(j * (feats // ND), feats // ND)
            d1[j] = Hop(down.at[:, at], dn.at[pl.ds(width, width), at], v_d.at[0, :, at], ahead)
            return [d1[j]]

        return 1, go

    def relay_d(hop, j):
        def go():
            source, made = (d1, d2) if hop == 2 else (d2, d3)
            arrive(source[j])
            at = pl.ds(j * (feats // ND), feats // ND)
            made[j] = Hop(
                dn.at[pl.ds((hop - 1) * width, width), at],
                dn.at[pl.ds(hop * width, width), at],
                v_d.at[hop - 1, :, at],
                ahead,
            )
            return [made[j]]

        return 1, go

    def send_a(store, i, at, count):
        def go():
            ds = (pl.ds(i * ra, ra), pl.ds(at, count))
            store[i] = Hop(acts.at[ds], a_1.at[ds], v_a1.at[ds], behind)
            return [store[i]]

        return ra * count / unit, go

    def relay_a(i):
        def go():
            arrive(a1n[i])
            ds = (pl.ds(i * ra, ra), pl.ds(0, near))
            to = pl.ds(i * ra, ra)
            a2[i] = Hop(a_1.at[ds], a_2.at[to], v_a2.at[to], behind)
            return [a2[i]]

        return ra * near / unit, go

    ahead_stream = [send_w(at) for at in range(near, feats, kw)]
    ahead_stream += [send_w(at) for at in range(0, near, kw)]
    ahead_stream += [relay_w(at) for at in range(near, feats, kw)]
    ahead_stream += [send_d(j) for j in range(ND)]
    ahead_stream += [relay_d(2, j) for j in range(ND)]
    ahead_stream += [relay_d(3, j) for j in range(ND)]
    back_stream = [send_a(a1n, i, 0, near) for i in range(NA)]
    back_stream += [relay_a(i) for i in range(NA)]
    back_stream += [send_a(a1f, i, near, far) for i in range(NA)]

    def weights(ref, at, kc):
        return [ref[0, pl.ds(at, kc), :], ref[1, pl.ds(at, kc), :]]

    def whole(a_ref, w_ref, count):
        kc = feats // 16
        acc[...] = jnp.zeros_like(acc)

        def step(k, _):
            at = pl.multiple_of(k * kc, kc)
            w = jnp.concatenate(weights(w_ref, at, kc), axis=1)
            acc[...] += dot(a_ref[:, pl.ds(at, kc)], w)
            return 0

        lax.fori_loop(0, count // kc, step, 0)

    def reduce_1(buf, into):
        return remote(buf.at[1 - core], into, twin)

    def reduce_2(copy, buf, into, half):
        arrive(copy)
        into[...] = into[...] + buf[core]
        return remote(into.at[1 - y], half, across)

    def reduce_3(copy, into, half):
        arrive(copy)
        return into[y] + half[...]

    def gather_1(at):
        return remote(hid.at[at], hid.at[at], twin), remote(hid.at[at], hid.at[at], across)

    def gather_2(copies, at):
        arrive(copies[1])
        return copies[0], remote(hid.at[at], hid.at[at], twin)

    todo = {}

    def when(step):
        def note(f):
            todo.setdefault(step, []).append(f)
            return f

        return note

    arrivals = []
    state = {}

    def own_at(s, block):
        at = pl.multiple_of(block * qr, qr)
        return pl.ds(at, qr), pl.ds(s * width, width)

    def own_pair(s, step, w_ref, ready):
        @when(step)
        def _():
            ready()
            whole(a_own, w_ref, feats)
            for q in range(4):
                part[s, q // 2, q % 2] = acc[q * qr : (q + 1) * qr, :]
            state["p", s] = reduce_1(part.at[s], part_in.at[s])

        @when(step + 1)
        def _():
            state["p", s] = reduce_2(state["p", s], part.at[s], part_in.at[s], half_in.at[s])

        @when(step + 1 + LAG)
        def _():
            total = reduce_3(state["p", s], part_in.at[s], half_in.at[s])
            hid[own_at(s, mine)] = silu_times(total[:, :width], total[:, width:]).astype(BF16)
            state["p", s] = gather_1(own_at(s, mine))

        @when(step + 1 + 2 * LAG)
        def _():
            arrivals.extend(gather_2(state["p", s], own_at(s, 2 * core + 1 - y)))

    def loaded():
        for c in loads:
            c.wait()

    def arrived():
        for cs in w1.values():
            for c in cs:
                arrive(c)

    size_w, size_a = feats * 2 * width / unit, rows * near / unit
    size_f = rows * far / unit
    step_1 = int(size_w) + crossed
    step_c = max(step_1 + 1, int(2 * size_a) + crossed)
    own_pair(0, 0, w_own, loaded)
    own_pair(1, step_1, w_1, arrived)

    @when(step_1)
    def _():
        for i in range(NA):
            arrive(a1n[i])
        whole(a_1, w_1, near)

    @when(step_c)
    def _():
        kc = feats // 16
        for i in range(NA):
            arrive(a2[i])
        for i in range(NB):

            def near_step(k, total, i=i):
                at = pl.multiple_of(k * kc, kc)
                w = jnp.concatenate(weights(w_1, at, kc), axis=1)
                return total + dot(a_2[pl.ds(i * rb, rb), pl.ds(at, kc)], w)

            total = lax.fori_loop(0, near // kc, near_step, jnp.zeros((rb, 2 * width), F32))
            for q in range(4):
                far_part[q // 2, q % 2, i] = total[q * rq : (q + 1) * rq, :]
        state["c"] = reduce_1(far_part, far_in)

    @when(step_c + 1)
    def _():
        state["c"] = reduce_2(state["c"], far_part, far_in, far_half)

    @when(step_c + 1 + LAG)
    def _():
        carry[...] = reduce_3(state["c"], far_in, far_half)
        state["c"] = Hop(carry, carry_in, v_carry, ahead)

    def stage_at(i, block):
        at = pl.multiple_of(i * rb + block * rq, rq)
        return pl.ds(at, rq), pl.ds(2 * width, 2 * width)

    def stage_a(i):
        kc = feats // 16
        for j in range(i * NA // NB, (i + 1) * NA // NB):
            arrive(a1f[j])
        if i == 0:
            for cs in w2.values():
                for c in cs:
                    arrive(c)

        def far_step(k, total):
            at = pl.multiple_of(k * kc, kc)
            there = pl.multiple_of(near + at, kc)
            w = jnp.concatenate(weights(w_1, there, kc) + weights(w_2, at, kc), axis=1)
            return total + dot(a_1[pl.ds(i * rb, rb), pl.ds(there, kc)], w)

        total = lax.fori_loop(0, far // kc, far_step, jnp.zeros((rb, 4 * width), F32))
        for q in range(4):
            this = total[q * rq : (q + 1) * rq, :]
            first = this[:, : 2 * width] + acc[pl.ds(i * rb + q * rq, rq), :]
            stage[i, q // 2, q % 2, :, : 2 * width] = first
            stage[i, q // 2, q % 2, :, 2 * width :] = this[:, 2 * width :]
        state["s", i] = reduce_1(stage.at[i], stage_in.at[i])

    def stage_b(i):
        state["s", i] = reduce_2(state["s", i], stage.at[i], stage_in.at[i], stage_half.at[i])

    def stage_c(i):
        if i == 0:
            state["c"].pass_on()
            arrive(state["c"])
        total = reduce_3(state["s", i], stage_in.at[i], stage_half.at[i])
        one, two = total[:, : 2 * width], total[:, 2 * width :] + carry_in[i]
        fwd[i, :, :width] = silu_times(one[:, :width], one[:, width:]).astype(BF16)
        fwd[i, :, width:] = silu_times(two[:, :width], two[:, width:]).astype(BF16)
        state["s", i] = Hop(
            fwd.at[i],
            hid.at[stage_at(i, mine)],
            v_fwd.at[i],
            ahead,
            hid.at[stage_at(i, 2 * core + 1 - y)],
        )

    def stage_d(i):
        state["s", i].pass_on()
        arrive(state["s", i])
        state["s", i] = gather_1(stage_at(i, mine))

    def stage_e(i):
        arrivals.extend(gather_2(state["s", i], stage_at(i, 2 * core + 1 - y)))

    last = int(2 * size_w - size_w * near / feats + 3 * ND) + 1
    for i in range(NB):
        step = int(2 * size_a + size_f * (i + 1) / NB) + crossed
        later = (0, 1, 1 + LAG, 1 + LAG + crossed, 1 + 2 * LAG + crossed)
        for f, j in zip((stage_a, stage_b, stage_c, stage_d, stage_e), later):
            when(min(step + j, last))(functools.partial(f, i))

    queues = []
    for stream in (ahead_stream, back_stream):
        due, total = [], 0.0
        for size, go in stream:
            due.append((int(total + 1e-6), go))
            total += size
        queues.append([due, 0, []])
    for step in range(last + 1):
        for queue in queues:
            due, place, sent = queue
            for copies in [c for at, c in sent if at == step - landed]:
                for c in copies:
                    c.pass_on()
            for copies in [c for at, c in sent if at == step - WINDOW]:
                for c in copies:
                    c.wait_send()
            while place < len(due) and due[place][0] <= step:
                sent.append((step, due[place][1]()))
                place += 1
            queue[1] = place
        for f in todo.get(step, []):
            f()
            if step == last:
                for c in hops:
                    c.pass_on()
        if step == last:
            for c in hops:
                c.pass_on()
    for due, place, _ in queues:
        assert place == len(due)
    assert len(started) <= COPIES

    for c in arrivals:
        arrive(c)
    stores = []
    for e in range(ND):
        arrive(d3[e])
        cols = feats // ND
        at = pl.ds(e * cols, cols)
        o_buf[:, at] = dot(hid[...], dn[:, at]).astype(BF16)
        c = pltpu.make_async_copy(o_buf.at[:, at], out.at[:, at], local_sem.at[4 + e])
        c.start()
        stores.append(c)
    waited = {id(c) for _, _, sent in queues for at, cs in sent if at + WINDOW <= last for c in cs}
    for c in started:
        if id(c) not in waited:
            c.wait_send()
    for c in hops:
        pl.when(c.via)(c.second.wait_send)
    for c in stores:
        c.wait()


def body(n, near, acts, gate, up, down):
    rows, feats = acts.shape
    width = gate.shape[1]
    far = feats - near
    rb, qr = rows // NB, rows // 4
    rq = rb // 4
    any_space = pl.BlockSpec(memory_space=pl.ANY)
    vmem = pltpu.VMEM
    return pl.pallas_call(
        functools.partial(kernel, n, near),
        out_shape=jax.ShapeDtypeStruct((rows, feats), BF16),
        in_specs=[any_space] * 4,
        out_specs=any_space,
        scratch_shapes=[
            vmem((rows, feats), BF16),
            vmem((rows, feats), BF16),
            vmem((rows, near), BF16),
            vmem((2, feats, width), BF16),
            vmem((2, feats, width), BF16),
            vmem((2, far, width), BF16),
            vmem((4 * width, feats), BF16),
            vmem((rows, 4 * width), BF16),
            vmem((2, 2, 2, qr, 2 * width), F32),
            vmem((2, 2, qr, 2 * width), F32),
            vmem((2, qr, 2 * width), F32),
            vmem((2, 2, NB, rq, 2 * width), F32),
            vmem((2, NB, rq, 2 * width), F32),
            vmem((NB, rq, 2 * width), F32),
            vmem((rows, 2 * width), F32),
            vmem((NB, 2, 2, rq, 4 * width), F32),
            vmem((NB, 2, rq, 4 * width), F32),
            vmem((NB, rq, 4 * width), F32),
            vmem((NB, rq, 2 * width), F32),
            vmem((NB, rq, 2 * width), F32),
            vmem((NB, rq, 2 * width), BF16),
            vmem((rows, feats), BF16),
            vmem((2, feats, width), BF16),
            vmem((2, far, width), BF16),
            vmem((3, width, feats), BF16),
            vmem((rows, feats), BF16),
            vmem((rows, near), BF16),
            vmem((NB, rq, 2 * width), F32),
            vmem((NB, rq, 2 * width), BF16),
            pltpu.SemaphoreType.DMA((COPIES,)),
            pltpu.SemaphoreType.DMA((COPIES,)),
            pltpu.SemaphoreType.DMA((COPIES,)),
            pltpu.SemaphoreType.DMA((COPIES,)),
            pltpu.SemaphoreType.DMA((4 + ND,)),
        ],
        compiler_params=pltpu.CompilerParams(
            collective_id=0, has_side_effects=True, vmem_limit_bytes=56 * 2**20
        ),
    )(acts, gate, up, down)


def solution(mesh):
    n = mesh.shape["loop"]
    placed = (P("loop", "rep"), P("rep", "loop"), P("rep", "loop"), P("loop", "rep"))

    def step(acts, gate, up, down):
        return body(n, acts.shape[1] // 16 * NEAR, acts, gate, up, down)

    return jax.shard_map(
        step, mesh=mesh, in_specs=placed, out_specs=P("loop", "rep"), check_vma=False
    )
```

```python
import functools

import jax
import jax.numpy as jnp
from jax import lax
from jax.experimental import pallas as pl
from jax.experimental.pallas import tpu as pltpu
from jax.sharding import PartitionSpec as P

MESH = pl.DeviceIdType.MESH
NA = 16
ND = 8
WINDOW = 3
PASS = 4
CROSS = 3
LAG = 5
COPIES = 136
F32 = jnp.float32
BF16 = jnp.bfloat16


def dot(a, b):
    return jnp.dot(a, b, preferred_element_type=F32)


def silu_times(gate, up):
    return gate / (1.0 + jnp.exp(-gate)) * up


def kernel(
    n,
    acts,
    gate,
    up,
    down,
    out,
    a_own,
    a_1,
    w_own,
    w_1,
    w_2,
    dn,
    hid,
    acc,
    part,
    part_in,
    half_in,
    fwd,
    o_buf,
    v_w1,
    v_w2,
    v_d,
    v_a1,
    v_fwd,
    send_sem,
    recv_sem,
    pass_sem,
    on_sem,
    local_sem,
):
    l, r = lax.axis_index("loop"), lax.axis_index("rep")
    core, y = lax.rem(r, 2), lax.div(r, 2)
    ahead = (lax.rem(l + 1, n), r)
    behind = (lax.rem(l + n - 1, n), r)
    half = n // 2
    first, final = lax.rem(l, half) == 0, lax.rem(l, half) == half - 1
    other = lax.rem(r + 2, 4)
    partner = (lax.rem(l + half, n), other)
    ahead_via = (lax.rem(l + 1 + half, n), other)
    behind_via = (lax.rem(l + n - 1 + half, n), other)
    ahead_other = (lax.rem(l + 1, n), other)
    behind_other = (lax.rem(l + n - 1, n), other)
    twin = (l, r + 1 - 2 * core)
    across = (l, lax.rem(r + 2, 4))
    rows, feats = acts.shape
    width = gate.shape[1]
    ra = rows // NA
    qr = rows // 4
    mine = 2 * core + y
    started = []

    def remote(src, dst, to):
        i = len(started)
        c = pltpu.make_async_remote_copy(
            src_ref=src,
            dst_ref=dst,
            send_sem=send_sem.at[i],
            recv_sem=recv_sem.at[i],
            device_id=to,
            device_id_type=MESH,
        )
        c.start()
        started.append(c)
        return c

    class Hop:
        def __init__(self, src, dst, by, to, on=None, mate=False):
            self.i = i = len(started)
            self.by, self.on = by, dst if on is None else on
            self.end, self.via = (final, first) if to is ahead else (first, final)
            self.partner = partner
            handed = ahead_via if to is ahead else behind_via
            if mate:
                self.via, handed, self.partner = final, across, ahead_other
            whole = pltpu.make_async_remote_copy(
                src_ref=src,
                dst_ref=dst,
                send_sem=send_sem.at[i],
                recv_sem=recv_sem.at[i],
                device_id=to,
                device_id_type=MESH,
            )
            leg = pltpu.make_async_remote_copy(
                src_ref=src,
                dst_ref=by,
                send_sem=send_sem.at[i],
                recv_sem=pass_sem.at[i],
                device_id=handed,
                device_id_type=MESH,
            )
            self.whole, self.leg = whole, leg
            pl.when(self.end)(leg.start)
            pl.when(jnp.logical_not(self.end))(whole.start)
            started.append(self)
            hops.append(self)

        def pass_on(self):
            if self in passed:
                return
            passed.append(self)
            second = pltpu.make_async_remote_copy(
                src_ref=self.by,
                dst_ref=self.on,
                send_sem=on_sem.at[self.i],
                recv_sem=recv_sem.at[self.i],
                device_id=self.partner,
                device_id_type=MESH,
            )
            self.second = second

            @pl.when(self.via)
            def _():
                self.leg.wait_recv()
                second.start()

        def wait_send(self):
            self.whole.wait_send()

        def wait_recv(self):
            self.whole.wait_recv()

    hops, passed = [], []
    here = set()

    def arrive(c):
        if id(c) not in here:
            here.add(id(c))
            c.wait_recv()

    loads = [
        pltpu.make_async_copy(acts, a_own, local_sem.at[0]),
        pltpu.make_async_copy(gate, w_own.at[0], local_sem.at[1]),
        pltpu.make_async_copy(up, w_own.at[1], local_sem.at[2]),
        pltpu.make_async_copy(down, dn.at[pl.ds(0, width)], local_sem.at[3]),
    ]
    for c in loads:
        c.start()

    barrier = pltpu.get_barrier_semaphore()
    def greet(p):
        pl.semaphore_signal(barrier, inc=1, device_id=p, device_id_type=MESH)

    def choose(cond, one, two):
        return tuple(jnp.where(cond, a, b) for a, b in zip(one, two))

    for p in (choose(final, ahead_via, ahead), choose(first, behind_via, behind), twin, across):
        greet(p)

    @pl.when(jnp.logical_or(first, final))
    def _():
        greet(partner)
        greet(choose(final, ahead_other, behind_other))
        pl.semaphore_wait(barrier, 6)

    @pl.when(jnp.logical_not(jnp.logical_or(first, final)))
    def _():
        pl.semaphore_wait(barrier, 4)

    crossed = PASS + CROSS
    unit = feats * width // ND
    kw = unit // (2 * width)
    w1, w2, d1, d2, d3 = {}, {}, {}, {}, {}
    a1 = {}

    def send_w(at):
        def go():
            ds = pl.ds(at, kw)
            w1[at] = [
                Hop(s.at[ds], w_1.at[h, ds], v_w1.at[h, ds], ahead) for h, s in enumerate((gate, up))
            ]
            return w1[at]

        return kw * 2 * width / unit, go

    def relay_w(at):
        def go():
            for c in w1[at]:
                arrive(c)
            src = dst = pl.ds(at, kw)
            w2[at] = [
                Hop(w_1.at[h, src], w_2.at[h, dst], v_w2.at[h, dst], ahead) for h in range(2)
            ]
            return w2[at]

        return kw * 2 * width / unit, go

    def send_d(j):
        def go():
            at = pl.ds(j * (feats // ND), feats // ND)
            d1[j] = Hop(down.at[:, at], dn.at[pl.ds(width, width), at], v_d.at[0, :, at], ahead, mate=j % 2 == 0)
            return [d1[j]]

        return 1, go

    def relay_d(hop, j):
        def go():
            source, made = (d1, d2) if hop == 2 else (d2, d3)
            arrive(source[j])
            at = pl.ds(j * (feats // ND), feats // ND)
            made[j] = Hop(
                dn.at[pl.ds((hop - 1) * width, width), at],
                dn.at[pl.ds(hop * width, width), at],
                v_d.at[hop - 1, :, at],
                ahead,
                mate=j % 2 == 0,
            )
            return [made[j]]

        return 1, go

    def send_a(i):
        def go():
            ds = pl.ds(i * ra, ra)
            a1[i] = Hop(acts.at[ds], a_1.at[ds], v_a1.at[ds], behind)
            return [a1[i]]

        return ra * feats / unit, go

    ahead_stream = [send_w(at) for at in range(0, feats, kw)]
    ahead_stream += [relay_w(at) for at in range(0, feats, kw)]
    ahead_stream += [send_d(j) for j in range(ND)]
    ahead_stream += [relay_d(2, j) for j in range(ND)]
    ahead_stream += [relay_d(3, j) for j in range(ND)]
    back_stream = [send_a(i) for i in range(NA)]

    def weights(ref, at, kc):
        return [ref[0, pl.ds(at, kc), :], ref[1, pl.ds(at, kc), :]]

    def whole(a_ref, w_ref):
        kc = feats // 16
        acc[...] = jnp.zeros_like(acc)

        def step(k, _):
            at = pl.multiple_of(k * kc, kc)
            w = jnp.concatenate(weights(w_ref, at, kc), axis=1)
            acc[...] += dot(a_ref[:, pl.ds(at, kc)], w)
            return 0

        lax.fori_loop(0, feats // kc, step, 0)

    def reduce_1(buf, into):
        return remote(buf.at[1 - core], into, twin)

    def reduce_2(copy, buf, into, half):
        arrive(copy)
        into[...] = into[...] + buf[core]
        return remote(into.at[1 - y], half, across)

    def reduce_3(copy, into, half):
        arrive(copy)
        return into[y] + half[...]

    def gather_1(at):
        return remote(hid.at[at], hid.at[at], twin), remote(hid.at[at], hid.at[at], across)

    def gather_2(copies, at):
        arrive(copies[1])
        return copies[0], remote(hid.at[at], hid.at[at], twin)

    todo = {}

    def when(step):
        def note(f):
            todo.setdefault(step, []).append(f)
            return f

        return note

    arrivals = []
    state = {}

    def spot(s, block):
        at = pl.multiple_of(block * qr, qr)
        return pl.ds(at, qr), pl.ds(s * width, width)

    theirs = 2 * core + 1 - y

    def pair(s, step, a_ref, w_ref, ready, late=None):
        steps = [step, step + 1 if late is None else late]
        steps += [steps[-1] + LAG]
        if s > 1:
            steps += [steps[-1] + crossed]
        steps += [steps[-1] + LAG]
        steps = [min(at, last) for at in steps]

        if s > 1 and steps[2] + PASS - 1 < steps[3]:
            when(steps[2] + PASS - 1)(lambda: state[s].pass_on())

        @when(steps[0])
        def _():
            ready()
            whole(a_ref, w_ref)
            for q in range(4):
                part[s, q // 2, q % 2] = acc[q * qr : (q + 1) * qr, :]
            state[s] = reduce_1(part.at[s], part_in.at[s])

        @when(steps[1])
        def _():
            state[s] = reduce_2(state[s], part.at[s], part_in.at[s], half_in.at[s])

        @when(steps[2])
        def _():
            total = reduce_3(state[s], part_in.at[s], half_in.at[s])
            value = silu_times(total[:, :width], total[:, width:]).astype(BF16)
            if s > 1:
                fwd[s - 2] = value
                state[s] = Hop(
                    fwd.at[s - 2], hid.at[spot(s, mine)], v_fwd.at[s - 2], ahead, hid.at[spot(s, theirs)]
                )
            else:
                hid[spot(s, mine)] = value
                state[s] = gather_1(spot(s, mine))

        if s > 1:

            @when(steps[3])
            def _():
                state[s].pass_on()
                arrive(state[s])
                state[s] = gather_1(spot(s, mine))

        @when(steps[-1])
        def _():
            arrivals.extend(gather_2(state[s], spot(s, theirs)))

    def loaded():
        for c in loads:
            c.wait()

    def of_w(w):
        def ready():
            for cs in w.values():
                for c in cs:
                    arrive(c)
            for c in a1.values():
                if w is w2:
                    arrive(c)

        return ready

    def of_a():
        for c in a1.values():
            arrive(c)

    size_w, size_a = feats * 2 * width / unit, rows * feats / unit
    last = int(2 * size_w + 3 * ND) + 1
    quiet = int(size_a) + 1
    pair(0, 0, a_own, w_own, loaded, quiet)
    pair(1, int(size_w) - 1 + crossed, a_own, w_1, of_w(w1), quiet + 2)
    pair(2, int(size_a) - 1 + crossed, a_1, w_1, of_a)
    pair(3, int(max(size_a, 2 * size_w)) + crossed, a_1, w_2, of_w(w2))

    queues = []
    for stream in (ahead_stream, back_stream):
        due, total = [], 0.0
        for size, go in stream:
            due.append((int(total + 1e-6), go))
            total += size
        queues.append([due, 0, []])
    for step in range(last + 1):
        for queue in queues:
            due, place, sent = queue
            for copies in [c for at, c in sent if at == step - PASS]:
                for c in copies:
                    c.pass_on()
            for copies in [c for at, c in sent if at == step - WINDOW]:
                for c in copies:
                    c.wait_send()
            while place < len(due) and due[place][0] <= step:
                sent.append((step, due[place][1]()))
                place += 1
            queue[1] = place
        for f in todo.get(step, []):
            f()
            if step == last:
                for c in hops:
                    c.pass_on()
        if step == last:
            for c in hops:
                c.pass_on()
    for due, place, _ in queues:
        assert place == len(due)
    assert len(started) <= COPIES

    for c in arrivals:
        arrive(c)
    stores = []
    for e in range(ND):
        arrive(d3[e])
        cols = feats // ND
        at = pl.ds(e * cols, cols)
        o_buf[:, at] = dot(hid[...], dn[:, at]).astype(BF16)
        c = pltpu.make_async_copy(o_buf.at[:, at], out.at[:, at], local_sem.at[4 + e])
        c.start()
        stores.append(c)
    waited = {id(c) for _, _, sent in queues for at, cs in sent if at + WINDOW <= last for c in cs}
    for c in started:
        if id(c) not in waited:
            c.wait_send()
    for c in hops:
        pl.when(c.via)(c.second.wait_send)
    for c in stores:
        c.wait()


def body(n, acts, gate, up, down):
    rows, feats = acts.shape
    width = gate.shape[1]
    qr = rows // 4
    any_space = pl.BlockSpec(memory_space=pl.ANY)
    vmem = pltpu.VMEM
    return pl.pallas_call(
        functools.partial(kernel, n),
        out_shape=jax.ShapeDtypeStruct((rows, feats), BF16),
        in_specs=[any_space] * 4,
        out_specs=any_space,
        scratch_shapes=[
            vmem((rows, feats), BF16),
            vmem((rows, feats), BF16),
            vmem((2, feats, width), BF16),
            vmem((2, feats, width), BF16),
            vmem((2, feats, width), BF16),
            vmem((4 * width, feats), BF16),
            vmem((rows, 4 * width), BF16),
            vmem((rows, 2 * width), F32),
            vmem((4, 2, 2, qr, 2 * width), F32),
            vmem((4, 2, qr, 2 * width), F32),
            vmem((4, qr, 2 * width), F32),
            vmem((2, qr, width), BF16),
            vmem((rows, feats), BF16),
            vmem((2, feats, width), BF16),
            vmem((2, feats, width), BF16),
            vmem((3, width, feats), BF16),
            vmem((rows, feats), BF16),
            vmem((2, qr, width), BF16),
            pltpu.SemaphoreType.DMA((COPIES,)),
            pltpu.SemaphoreType.DMA((COPIES,)),
            pltpu.SemaphoreType.DMA((COPIES,)),
            pltpu.SemaphoreType.DMA((COPIES,)),
            pltpu.SemaphoreType.DMA((4 + ND,)),
        ],
        compiler_params=pltpu.CompilerParams(
            collective_id=0, has_side_effects=True, vmem_limit_bytes=56 * 2**20
        ),
    )(acts, gate, up, down)


def solution(mesh):
    n = mesh.shape["loop"]
    placed = (P("loop", "rep"), P("rep", "loop"), P("rep", "loop"), P("loop", "rep"))

    step = functools.partial(body, n)

    return jax.shard_map(
        step, mesh=mesh, in_specs=placed, out_specs=P("loop", "rep"), check_vma=False
    )
```

```python
import functools

import jax
import jax.numpy as jnp
from jax import lax
from jax.experimental import pallas as pl
from jax.experimental.pallas import tpu as pltpu
from jax.sharding import PartitionSpec as P

MESH = pl.DeviceIdType.MESH
NA = 16
ND = 8
WINDOW = 4
PASS = 3
CROSS = 4
LAG = 5
COPIES = 136
F32 = jnp.float32
BF16 = jnp.bfloat16


def dot(a, b):
    return jnp.dot(a, b, preferred_element_type=F32)


def silu_times(gate, up):
    return gate / (1.0 + jnp.exp(-gate)) * up


def kernel(
    n,
    acts,
    gate,
    up,
    down,
    out,
    a_own,
    a_1,
    w_own,
    w_1,
    w_2,
    dn,
    hid,
    acc,
    part,
    part_in,
    half_in,
    fwd,
    o_buf,
    v_w1,
    v_w2,
    v_d,
    v_a1,
    v_fwd,
    send_sem,
    recv_sem,
    pass_sem,
    on_sem,
    local_sem,
):
    l, r = lax.axis_index("loop"), lax.axis_index("rep")
    core, y = lax.rem(r, 2), lax.div(r, 2)
    ahead = (lax.rem(l + 1, n), r)
    behind = (lax.rem(l + n - 1, n), r)
    half = n // 2
    first, final = lax.rem(l, half) == 0, lax.rem(l, half) == half - 1
    other = lax.rem(r + 2, 4)
    partner = (lax.rem(l + half, n), other)
    ahead_via = (lax.rem(l + 1 + half, n), other)
    behind_via = (lax.rem(l + n - 1 + half, n), other)
    ahead_other = (lax.rem(l + 1, n), other)
    behind_other = (lax.rem(l + n - 1, n), other)
    twin = (l, r + 1 - 2 * core)
    across = (l, lax.rem(r + 2, 4))
    rows, feats = acts.shape
    width = gate.shape[1]
    ra = rows // NA
    qr = rows // 4
    mine = 2 * core + y
    started = []

    def remote(src, dst, to):
        i = len(started)
        c = pltpu.make_async_remote_copy(
            src_ref=src,
            dst_ref=dst,
            send_sem=send_sem.at[i],
            recv_sem=recv_sem.at[i],
            device_id=to,
            device_id_type=MESH,
        )
        c.start()
        started.append(c)
        return c

    class Hop:
        def __init__(self, src, dst, by, to, on=None, mate=False):
            self.i = i = len(started)
            self.by, self.on = by, dst if on is None else on
            self.end, self.via = (final, first) if to is ahead else (first, final)
            self.partner = partner
            handed = ahead_via if to is ahead else behind_via
            if mate:
                self.via, handed, self.partner = final, across, ahead_other
            whole = pltpu.make_async_remote_copy(
                src_ref=src,
                dst_ref=dst,
                send_sem=send_sem.at[i],
                recv_sem=recv_sem.at[i],
                device_id=to,
                device_id_type=MESH,
            )
            leg = pltpu.make_async_remote_copy(
                src_ref=src,
                dst_ref=by,
                send_sem=send_sem.at[i],
                recv_sem=pass_sem.at[i],
                device_id=handed,
                device_id_type=MESH,
            )
            self.whole, self.leg = whole, leg
            pl.when(self.end)(leg.start)
            pl.when(jnp.logical_not(self.end))(whole.start)
            started.append(self)
            hops.append(self)

        def pass_on(self):
            if self in passed:
                return
            passed.append(self)
            second = pltpu.make_async_remote_copy(
                src_ref=self.by,
                dst_ref=self.on,
                send_sem=on_sem.at[self.i],
                recv_sem=recv_sem.at[self.i],
                device_id=self.partner,
                device_id_type=MESH,
            )
            self.second = second

            @pl.when(self.via)
            def _():
                self.leg.wait_recv()
                second.start()

        def wait_send(self):
            self.whole.wait_send()

        def wait_recv(self):
            self.whole.wait_recv()

    hops, passed = [], []
    here = set()

    def arrive(c):
        if id(c) not in here:
            here.add(id(c))
            c.wait_recv()

    loads = [
        pltpu.make_async_copy(acts, a_own, local_sem.at[0]),
        pltpu.make_async_copy(gate, w_own.at[0], local_sem.at[1]),
        pltpu.make_async_copy(up, w_own.at[1], local_sem.at[2]),
        pltpu.make_async_copy(down, dn.at[pl.ds(0, width)], local_sem.at[3]),
    ]
    for c in loads:
        c.start()

    barrier = pltpu.get_barrier_semaphore()
    def greet(p):
        pl.semaphore_signal(barrier, inc=1, device_id=p, device_id_type=MESH)

    def choose(cond, one, two):
        return tuple(jnp.where(cond, a, b) for a, b in zip(one, two))

    for p in (choose(final, ahead_via, ahead), choose(first, behind_via, behind), twin, across):
        greet(p)

    @pl.when(jnp.logical_or(first, final))
    def _():
        greet(partner)
        greet(choose(final, ahead_other, behind_other))
        pl.semaphore_wait(barrier, 6)

    @pl.when(jnp.logical_not(jnp.logical_or(first, final)))
    def _():
        pl.semaphore_wait(barrier, 4)

    crossed = PASS + CROSS
    unit = feats * width // ND
    kw = unit // (2 * width)
    w1, w2, d1, d2, d3 = {}, {}, {}, {}, {}
    a1 = {}

    def send_w(at):
        def go():
            ds = pl.ds(at, kw)
            w1[at] = [
                Hop(s.at[ds], w_1.at[h, ds], v_w1.at[h, ds], ahead) for h, s in enumerate((gate, up))
            ]
            return w1[at]

        return kw * 2 * width / unit, go

    def relay_w(at):
        def go():
            for c in w1[at]:
                arrive(c)
            src = dst = pl.ds(at, kw)
            w2[at] = [
                Hop(w_1.at[h, src], w_2.at[h, dst], v_w2.at[h, dst], ahead) for h in range(2)
            ]
            return w2[at]

        return kw * 2 * width / unit, go

    def send_d(j):
        def go():
            at = pl.ds(j * (feats // ND), feats // ND)
            d1[j] = Hop(down.at[:, at], dn.at[pl.ds(width, width), at], v_d.at[0, :, at], ahead, mate=j % 2 == 0)
            return [d1[j]]

        return 1, go

    def relay_d(hop, j):
        def go():
            source, made = (d1, d2) if hop == 2 else (d2, d3)
            arrive(source[j])
            at = pl.ds(j * (feats // ND), feats // ND)
            made[j] = Hop(
                dn.at[pl.ds((hop - 1) * width, width), at],
                dn.at[pl.ds(hop * width, width), at],
                v_d.at[hop - 1, :, at],
                ahead,
                mate=j % 2 == 0,
            )
            return [made[j]]

        return 1, go

    def send_a(i):
        def go():
            ds = pl.ds(i * ra, ra)
            a1[i] = Hop(acts.at[ds], a_1.at[ds], v_a1.at[ds], behind)
            return [a1[i]]

        return ra * feats / unit, go

    ahead_stream = [send_w(at) for at in range(0, feats, kw)]
    ahead_stream += [relay_w(at) for at in range(0, feats, kw)]
    ahead_stream += [send_d(j) for j in range(ND)]
    ahead_stream += [relay_d(2, j) for j in range(ND)]
    ahead_stream += [relay_d(3, j) for j in range(ND)]
    back_stream = [send_a(i) for i in range(NA)]

    def weights(ref, at, kc):
        return [ref[0, pl.ds(at, kc), :], ref[1, pl.ds(at, kc), :]]

    def whole(a_ref, w_ref):
        kc = feats // 16
        acc[...] = jnp.zeros_like(acc)

        def step(k, _):
            at = pl.multiple_of(k * kc, kc)
            w = jnp.concatenate(weights(w_ref, at, kc), axis=1)
            acc[...] += dot(a_ref[:, pl.ds(at, kc)], w)
            return 0

        lax.fori_loop(0, feats // kc, step, 0)

    def reduce_1(buf, into):
        return remote(buf.at[1 - core], into, twin)

    def reduce_2(copy, buf, into, half):
        arrive(copy)
        into[...] = into[...] + buf[core]
        return remote(into.at[1 - y], half, across)

    def reduce_3(copy, into, half):
        arrive(copy)
        return into[y] + half[...]

    def gather_1(at):
        return remote(hid.at[at], hid.at[at], twin), remote(hid.at[at], hid.at[at], across)

    def gather_2(copies, at):
        arrive(copies[1])
        return copies[0], remote(hid.at[at], hid.at[at], twin)

    todo = {}

    def when(step):
        def note(f):
            todo.setdefault(step, []).append(f)
            return f

        return note

    arrivals = []
    state = {}

    def spot(s, block):
        at = pl.multiple_of(block * qr, qr)
        return pl.ds(at, qr), pl.ds(s * width, width)

    theirs = 2 * core + 1 - y

    def pair(s, step, a_ref, w_ref, ready, late=None):
        steps = [step, step + 1 if late is None else late]
        steps += [steps[-1] + LAG]
        if s > 1:
            steps += [steps[-1] + crossed]
        steps += [steps[-1] + LAG]
        steps = [min(at, last) for at in steps]

        if s > 1 and steps[2] + PASS - 1 < steps[3]:
            when(steps[2] + PASS - 1)(lambda: state[s].pass_on())

        @when(steps[0])
        def _():
            ready()
            whole(a_ref, w_ref)
            for q in range(4):
                part[s, q // 2, q % 2] = acc[q * qr : (q + 1) * qr, :]
            state[s] = reduce_1(part.at[s], part_in.at[s])

        @when(steps[1])
        def _():
            state[s] = reduce_2(state[s], part.at[s], part_in.at[s], half_in.at[s])

        @when(steps[2])
        def _():
            total = reduce_3(state[s], part_in.at[s], half_in.at[s])
            value = silu_times(total[:, :width], total[:, width:]).astype(BF16)
            if s > 1:
                fwd[s - 2] = value
                state[s] = Hop(
                    fwd.at[s - 2], hid.at[spot(s, mine)], v_fwd.at[s - 2], ahead, hid.at[spot(s, theirs)]
                )
            else:
                hid[spot(s, mine)] = value
                state[s] = gather_1(spot(s, mine))

        if s > 1:

            @when(steps[3])
            def _():
                state[s].pass_on()
                arrive(state[s])
                state[s] = gather_1(spot(s, mine))

        @when(steps[-1])
        def _():
            arrivals.extend(gather_2(state[s], spot(s, theirs)))

    def loaded():
        for c in loads:
            c.wait()

    def of_w(w):
        def ready():
            for cs in w.values():
                for c in cs:
                    arrive(c)
            for c in a1.values():
                if w is w2:
                    arrive(c)

        return ready

    def of_a():
        for c in a1.values():
            arrive(c)

    size_w, size_a = feats * 2 * width / unit, rows * feats / unit
    last = int(2 * size_w + 3 * ND) + 1
    quiet = int(size_a) + 1
    pair(0, 0, a_own, w_own, loaded, quiet)
    pair(1, int(size_w) - 1 + crossed, a_own, w_1, of_w(w1), quiet + 2)
    pair(2, int(size_a) - 1 + crossed, a_1, w_1, of_a)
    pair(3, int(max(size_a, 2 * size_w)) + crossed, a_1, w_2, of_w(w2))

    queues = []
    for stream in (ahead_stream, back_stream):
        due, total = [], 0.0
        for size, go in stream:
            due.append((int(total + 1e-6), go))
            total += size
        queues.append([due, 0, []])
    for step in range(last + 1):
        for queue in queues:
            due, place, sent = queue
            for copies in [c for at, c in sent if at == step - PASS]:
                for c in copies:
                    c.pass_on()
            for copies in [c for at, c in sent if at == step - WINDOW]:
                for c in copies:
                    c.wait_send()
            while place < len(due) and due[place][0] <= step:
                sent.append((step, due[place][1]()))
                place += 1
            queue[1] = place
        for f in todo.get(step, []):
            f()
            if step == last:
                for c in hops:
                    c.pass_on()
        if step == last:
            for c in hops:
                c.pass_on()
    for due, place, _ in queues:
        assert place == len(due)
    assert len(started) <= COPIES

    for c in arrivals:
        arrive(c)
    stores = []
    for e in range(ND):
        arrive(d3[e])
        cols = feats // ND
        at = pl.ds(e * cols, cols)
        o_buf[:, at] = dot(hid[...], dn[:, at]).astype(BF16)
        c = pltpu.make_async_copy(o_buf.at[:, at], out.at[:, at], local_sem.at[4 + e])
        c.start()
        stores.append(c)
    waited = {id(c) for _, _, sent in queues for at, cs in sent if at + WINDOW <= last for c in cs}
    for c in started:
        if id(c) not in waited:
            c.wait_send()
    for c in hops:
        pl.when(c.via)(c.second.wait_send)
    for c in stores:
        c.wait()


def body(n, acts, gate, up, down):
    rows, feats = acts.shape
    width = gate.shape[1]
    qr = rows // 4
    any_space = pl.BlockSpec(memory_space=pl.ANY)
    vmem = pltpu.VMEM
    return pl.pallas_call(
        functools.partial(kernel, n),
        out_shape=jax.ShapeDtypeStruct((rows, feats), BF16),
        in_specs=[any_space] * 4,
        out_specs=any_space,
        scratch_shapes=[
            vmem((rows, feats), BF16),
            vmem((rows, feats), BF16),
            vmem((2, feats, width), BF16),
            vmem((2, feats, width), BF16),
            vmem((2, feats, width), BF16),
            vmem((4 * width, feats), BF16),
            vmem((rows, 4 * width), BF16),
            vmem((rows, 2 * width), F32),
            vmem((4, 2, 2, qr, 2 * width), F32),
            vmem((4, 2, qr, 2 * width), F32),
            vmem((4, qr, 2 * width), F32),
            vmem((2, qr, width), BF16),
            vmem((rows, feats), BF16),
            vmem((2, feats, width), BF16),
            vmem((2, feats, width), BF16),
            vmem((3, width, feats), BF16),
            vmem((rows, feats), BF16),
            vmem((2, qr, width), BF16),
            pltpu.SemaphoreType.DMA((COPIES,)),
            pltpu.SemaphoreType.DMA((COPIES,)),
            pltpu.SemaphoreType.DMA((COPIES,)),
            pltpu.SemaphoreType.DMA((COPIES,)),
            pltpu.SemaphoreType.DMA((4 + ND,)),
        ],
        compiler_params=pltpu.CompilerParams(
            collective_id=0, has_side_effects=True, vmem_limit_bytes=56 * 2**20
        ),
    )(acts, gate, up, down)


def solution(mesh):
    n = mesh.shape["loop"]
    placed = (P("loop", "rep"), P("rep", "loop"), P("rep", "loop"), P("loop", "rep"))

    step = functools.partial(body, n)

    return jax.shard_map(
        step, mesh=mesh, in_specs=placed, out_specs=P("loop", "rep"), check_vma=False
    )
```

```python
import functools

import jax
import jax.numpy as jnp
from jax import lax
from jax.experimental import pallas as pl
from jax.experimental.pallas import tpu as pltpu
from jax.sharding import PartitionSpec as P

MESH = pl.DeviceIdType.MESH
NA = 16
ND = 8
NE = 16
WINDOW = 4
PASS = 3
CROSS = 4
LAG = 5
COPIES = 136
F32 = jnp.float32
BF16 = jnp.bfloat16


def dot(a, b):
    return jnp.dot(a, b, preferred_element_type=F32)


def silu_times(gate, up):
    return gate / (1.0 + jnp.exp(-gate)) * up


def kernel(
    n,
    acts,
    gate,
    up,
    down,
    out,
    a_own,
    a_1,
    w_own,
    w_1,
    w_2,
    dn,
    hid,
    acc,
    part,
    part_in,
    half_in,
    fwd,
    o_buf,
    v_w1,
    v_w2,
    v_d,
    v_a1,
    v_fwd,
    send_sem,
    recv_sem,
    pass_sem,
    on_sem,
    local_sem,
):
    l, r = lax.axis_index("loop"), lax.axis_index("rep")
    core, y = lax.rem(r, 2), lax.div(r, 2)
    ahead = (lax.rem(l + 1, n), r)
    behind = (lax.rem(l + n - 1, n), r)
    half = n // 2
    first, final = lax.rem(l, half) == 0, lax.rem(l, half) == half - 1
    other = lax.rem(r + 2, 4)
    partner = (lax.rem(l + half, n), other)
    ahead_via = (lax.rem(l + 1 + half, n), other)
    behind_via = (lax.rem(l + n - 1 + half, n), other)
    ahead_other = (lax.rem(l + 1, n), other)
    behind_other = (lax.rem(l + n - 1, n), other)
    twin = (l, r + 1 - 2 * core)
    across = (l, lax.rem(r + 2, 4))
    rows, feats = acts.shape
    width = gate.shape[1]
    ra = rows // NA
    qr = rows // 4
    mine = 2 * core + y
    started = []

    def remote(src, dst, to):
        i = len(started)
        c = pltpu.make_async_remote_copy(
            src_ref=src,
            dst_ref=dst,
            send_sem=send_sem.at[i],
            recv_sem=recv_sem.at[i],
            device_id=to,
            device_id_type=MESH,
        )
        c.start()
        started.append(c)
        return c

    class Hop:
        def __init__(self, src, dst, by, to, on=None, mate=False):
            self.i = i = len(started)
            self.by, self.on = by, dst if on is None else on
            self.end, self.via = (final, first) if to is ahead else (first, final)
            self.partner = partner
            handed = ahead_via if to is ahead else behind_via
            if mate:
                self.via, handed, self.partner = final, across, ahead_other
            whole = pltpu.make_async_remote_copy(
                src_ref=src,
                dst_ref=dst,
                send_sem=send_sem.at[i],
                recv_sem=recv_sem.at[i],
                device_id=to,
                device_id_type=MESH,
            )
            leg = pltpu.make_async_remote_copy(
                src_ref=src,
                dst_ref=by,
                send_sem=send_sem.at[i],
                recv_sem=pass_sem.at[i],
                device_id=handed,
                device_id_type=MESH,
            )
            self.whole, self.leg = whole, leg
            pl.when(self.end)(leg.start)
            pl.when(jnp.logical_not(self.end))(whole.start)
            started.append(self)
            hops.append(self)

        def pass_on(self):
            if self in passed:
                return
            passed.append(self)
            second = pltpu.make_async_remote_copy(
                src_ref=self.by,
                dst_ref=self.on,
                send_sem=on_sem.at[self.i],
                recv_sem=recv_sem.at[self.i],
                device_id=self.partner,
                device_id_type=MESH,
            )
            self.second = second

            @pl.when(self.via)
            def _():
                self.leg.wait_recv()
                second.start()

        def wait_send(self):
            self.whole.wait_send()

        def wait_recv(self):
            self.whole.wait_recv()

    hops, passed = [], []
    here = set()

    def arrive(c):
        if id(c) not in here:
            here.add(id(c))
            c.wait_recv()

    loads = [
        pltpu.make_async_copy(acts, a_own, local_sem.at[0]),
        pltpu.make_async_copy(gate, w_own.at[0], local_sem.at[1]),
        pltpu.make_async_copy(up, w_own.at[1], local_sem.at[2]),
        pltpu.make_async_copy(down, dn.at[pl.ds(0, width)], local_sem.at[3]),
    ]
    for c in loads:
        c.start()

    barrier = pltpu.get_barrier_semaphore()
    def greet(p):
        pl.semaphore_signal(barrier, inc=1, device_id=p, device_id_type=MESH)

    def choose(cond, one, two):
        return tuple(jnp.where(cond, a, b) for a, b in zip(one, two))

    for p in (choose(final, ahead_via, ahead), choose(first, behind_via, behind), twin, across):
        greet(p)

    @pl.when(jnp.logical_or(first, final))
    def _():
        greet(partner)
        greet(choose(final, ahead_other, behind_other))
        pl.semaphore_wait(barrier, 6)

    @pl.when(jnp.logical_not(jnp.logical_or(first, final)))
    def _():
        pl.semaphore_wait(barrier, 4)

    crossed = PASS + CROSS
    unit = feats * width // ND
    kw = unit // (2 * width)
    w1, w2, d1, d2, d3 = {}, {}, {}, {}, {}
    a1 = {}

    def send_w(at):
        def go():
            ds = pl.ds(at, kw)
            w1[at] = [
                Hop(s.at[ds], w_1.at[h, ds], v_w1.at[h, ds], ahead) for h, s in enumerate((gate, up))
            ]
            return w1[at]

        return kw * 2 * width / unit, go

    def relay_w(at):
        def go():
            for c in w1[at]:
                arrive(c)
            src = dst = pl.ds(at, kw)
            w2[at] = [
                Hop(w_1.at[h, src], w_2.at[h, dst], v_w2.at[h, dst], ahead) for h in range(2)
            ]
            return w2[at]

        return kw * 2 * width / unit, go

    def send_d(j):
        def go():
            at = pl.ds(j * (feats // ND), feats // ND)
            d1[j] = Hop(down.at[:, at], dn.at[pl.ds(width, width), at], v_d.at[0, :, at], ahead, mate=j % 2 == 0)
            return [d1[j]]

        return 1, go

    def relay_d(hop, j, count):
        def go():
            source, made = (d1, d2) if hop == 2 else (d2, d3)
            arrive(source[j * ND // count])
            at = pl.ds(j * (feats // count), feats // count)
            made[j] = Hop(
                dn.at[pl.ds((hop - 1) * width, width), at],
                dn.at[pl.ds(hop * width, width), at],
                v_d.at[hop - 1, :, at],
                ahead,
                mate=j % 2 == 0,
            )
            return [made[j]]

        return ND / count, go

    def send_a(i):
        def go():
            ds = pl.ds(i * ra, ra)
            a1[i] = Hop(acts.at[ds], a_1.at[ds], v_a1.at[ds], behind)
            return [a1[i]]

        return ra * feats / unit, go

    ahead_stream = [send_w(at) for at in range(0, feats, kw)]
    ahead_stream += [relay_w(at) for at in range(0, feats, kw)]
    ahead_stream += [send_d(j) for j in range(ND)]
    ahead_stream += [relay_d(2, j, ND) for j in range(ND)]
    ahead_stream += [relay_d(3, j, NE) for j in range(NE)]
    back_stream = [send_a(i) for i in range(NA)]

    def weights(ref, at, kc):
        return [ref[0, pl.ds(at, kc), :], ref[1, pl.ds(at, kc), :]]

    def whole(a_ref, w_ref):
        kc = feats // 16
        acc[...] = jnp.zeros_like(acc)

        def step(k, _):
            at = pl.multiple_of(k * kc, kc)
            w = jnp.concatenate(weights(w_ref, at, kc), axis=1)
            acc[...] += dot(a_ref[:, pl.ds(at, kc)], w)
            return 0

        lax.fori_loop(0, feats // kc, step, 0)

    def reduce_1(buf, into):
        return remote(buf.at[1 - core], into, twin)

    def reduce_2(copy, buf, into, half):
        arrive(copy)
        into[...] = into[...] + buf[core]
        return remote(into.at[1 - y], half, across)

    def reduce_3(copy, into, half):
        arrive(copy)
        return into[y] + half[...]

    def gather_1(at):
        return remote(hid.at[at], hid.at[at], twin), remote(hid.at[at], hid.at[at], across)

    def gather_2(copies, at):
        arrive(copies[1])
        return copies[0], remote(hid.at[at], hid.at[at], twin)

    todo = {}

    def when(step):
        def note(f):
            todo.setdefault(step, []).append(f)
            return f

        return note

    arrivals = []
    state = {}

    def spot(s, block):
        at = pl.multiple_of(block * qr, qr)
        return pl.ds(at, qr), pl.ds(s * width, width)

    theirs = 2 * core + 1 - y

    def pair(s, step, a_ref, w_ref, ready, late=None):
        steps = [step, step + 1 if late is None else late]
        steps += [steps[-1] + LAG]
        if s > 1:
            steps += [steps[-1] + crossed]
        steps += [steps[-1] + LAG]
        steps = [min(at, last) for at in steps]

        if s > 1 and steps[2] + PASS - 1 < steps[3]:
            when(steps[2] + PASS - 1)(lambda: state[s].pass_on())

        @when(steps[0])
        def _():
            ready()
            whole(a_ref, w_ref)
            for q in range(4):
                part[s, q // 2, q % 2] = acc[q * qr : (q + 1) * qr, :]
            state[s] = reduce_1(part.at[s], part_in.at[s])

        @when(steps[1])
        def _():
            state[s] = reduce_2(state[s], part.at[s], part_in.at[s], half_in.at[s])

        @when(steps[2])
        def _():
            total = reduce_3(state[s], part_in.at[s], half_in.at[s])
            value = silu_times(total[:, :width], total[:, width:]).astype(BF16)
            if s > 1:
                fwd[s - 2] = value
                state[s] = Hop(
                    fwd.at[s - 2], hid.at[spot(s, mine)], v_fwd.at[s - 2], ahead, hid.at[spot(s, theirs)]
                )
            else:
                hid[spot(s, mine)] = value
                state[s] = gather_1(spot(s, mine))

        if s > 1:

            @when(steps[3])
            def _():
                state[s].pass_on()
                arrive(state[s])
                state[s] = gather_1(spot(s, mine))

        @when(steps[-1])
        def _():
            arrivals.extend(gather_2(state[s], spot(s, theirs)))

    def loaded():
        for c in loads:
            c.wait()

    def of_w(w):
        def ready():
            for cs in w.values():
                for c in cs:
                    arrive(c)
            for c in a1.values():
                if w is w2:
                    arrive(c)

        return ready

    def of_a():
        for c in a1.values():
            arrive(c)

    size_w, size_a = feats * 2 * width / unit, rows * feats / unit
    last = int(2 * size_w + 3 * ND) + 1
    quiet = int(size_a) + 1
    pair(0, 0, a_own, w_own, loaded, quiet)
    pair(1, int(size_w) - 1 + crossed, a_own, w_1, of_w(w1), quiet + 2)
    pair(2, int(size_a) - 1 + crossed, a_1, w_1, of_a)
    pair(3, int(max(size_a, 2 * size_w)) + crossed, a_1, w_2, of_w(w2))

    queues = []
    for stream in (ahead_stream, back_stream):
        due, total = [], 0.0
        for size, go in stream:
            due.append((int(total + 1e-6), go))
            total += size
        queues.append([due, 0, []])
    for step in range(last + 1):
        for queue in queues:
            due, place, sent = queue
            for copies in [c for at, c in sent if at == step - PASS]:
                for c in copies:
                    c.pass_on()
            for copies in [c for at, c in sent if at == step - WINDOW]:
                for c in copies:
                    c.wait_send()
            while place < len(due) and due[place][0] <= step:
                sent.append((step, due[place][1]()))
                place += 1
            queue[1] = place
        for f in todo.get(step, []):
            f()
            if step == last:
                for c in hops:
                    c.pass_on()
        if step == last:
            for c in hops:
                c.pass_on()
    for due, place, _ in queues:
        assert place == len(due)
    assert len(started) <= COPIES

    for c in arrivals:
        arrive(c)
    stores = []
    for e in range(NE):
        arrive(d3[e])
        cols = feats // NE
        at = pl.ds(e * cols, cols)
        o_buf[:, at] = dot(hid[...], dn[:, at]).astype(BF16)
        c = pltpu.make_async_copy(o_buf.at[:, at], out.at[:, at], local_sem.at[4 + e])
        c.start()
        stores.append(c)
    waited = {id(c) for _, _, sent in queues for at, cs in sent if at + WINDOW <= last for c in cs}
    for c in started:
        if id(c) not in waited:
            c.wait_send()
    for c in hops:
        pl.when(c.via)(c.second.wait_send)
    for c in stores:
        c.wait()


def body(n, acts, gate, up, down):
    rows, feats = acts.shape
    width = gate.shape[1]
    qr = rows // 4
    any_space = pl.BlockSpec(memory_space=pl.ANY)
    vmem = pltpu.VMEM
    return pl.pallas_call(
        functools.partial(kernel, n),
        out_shape=jax.ShapeDtypeStruct((rows, feats), BF16),
        in_specs=[any_space] * 4,
        out_specs=any_space,
        scratch_shapes=[
            vmem((rows, feats), BF16),
            vmem((rows, feats), BF16),
            vmem((2, feats, width), BF16),
            vmem((2, feats, width), BF16),
            vmem((2, feats, width), BF16),
            vmem((4 * width, feats), BF16),
            vmem((rows, 4 * width), BF16),
            vmem((rows, 2 * width), F32),
            vmem((4, 2, 2, qr, 2 * width), F32),
            vmem((4, 2, qr, 2 * width), F32),
            vmem((4, qr, 2 * width), F32),
            vmem((2, qr, width), BF16),
            vmem((rows, feats), BF16),
            vmem((2, feats, width), BF16),
            vmem((2, feats, width), BF16),
            vmem((3, width, feats), BF16),
            vmem((rows, feats), BF16),
            vmem((2, qr, width), BF16),
            pltpu.SemaphoreType.DMA((COPIES,)),
            pltpu.SemaphoreType.DMA((COPIES,)),
            pltpu.SemaphoreType.DMA((COPIES,)),
            pltpu.SemaphoreType.DMA((COPIES,)),
            pltpu.SemaphoreType.DMA((4 + NE,)),
        ],
        compiler_params=pltpu.CompilerParams(
            collective_id=0, has_side_effects=True, vmem_limit_bytes=56 * 2**20
        ),
    )(acts, gate, up, down)


def solution(mesh):
    n = mesh.shape["loop"]
    placed = (P("loop", "rep"), P("rep", "loop"), P("rep", "loop"), P("loop", "rep"))

    step = functools.partial(body, n)

    return jax.shard_map(
        step, mesh=mesh, in_specs=placed, out_specs=P("loop", "rep"), check_vma=False
    )
```
